32 devices in a mesh: tile: 4 (over z), src: 8 (over y, x, core).
Axes of the slice: x: 2, y: 2, z: 4, core: 2. Of those that a mesh axis runs over, the one named last changes fastest.
Arguments:
- permittivity: float32 [64, 16, 320], P(('tile', 'src')), may hold values from 1 to 2
- e_start: float32 [8, 3, 64, 16, 320], P('src', None, 'tile'), may hold values from -6 to 6
- h_start: float32 [8, 3, 64, 16, 320], P('src', None, 'tile'), may hold values from -6 to 6
- e_cotangent: float32 [8, 3, 64, 16, 320], P('src', None, 'tile'), may hold values from -6 to 6
- h_cotangent: float32 [8, 3, 64, 16, 320], P('src', None, 'tile'), may hold values from -6 to 6
Outputs:
- e_final: float32 [8, 3, 64, 16, 320], P('src', None, 'tile')
- gradient: float32 [64, 16, 320], P(('tile', 'src'))
The draws below stay inside these ranges and needn't reach their ends.
All inputs are finite; a program needn't handle non-finite values.
Results may differ from the reference program's by a relative error of at most 0.00002.
Values sent between devices are 32-bit elements; how exact they have to be, the bound alone decides.
A program may use at most 64 MiB of HBM per device.

```python
import math
import jax
import jax.numpy as jnp
from jax import lax

NY = 16
NZ = 320
STEPS = 6
SOURCES = 8
NX = 64


def spiked(array, key, source, target, parts, factor):
    def block_of(dim):
        return (jnp.arange(array.shape[dim]) // (array.shape[dim] // parts)).reshape((-1,) + (1,) * (array.ndim - 1 - dim))

    near = jax.random.permutation(key, parts)[block_of(target)]
    far = (block_of(target) + parts // 2) % parts
    return jnp.where((block_of(source) == near) | (block_of(source) == far), factor * array, array)


def shard_levels(stream_key, shape, shards, smallest, high):
    factor_of, own = 1.0, jax.random.fold_in(stream_key, 6)
    for position, shards_of in shards:
        heights = jnp.exp(jax.random.uniform(jax.random.fold_in(own, position), (shards_of,), jnp.float32, smallest / len(shards), high / len(shards)))
        factor_of = factor_of * jnp.repeat(heights, shape[position] // shards_of).reshape([-1 if axis == position else 1 for axis in range(len(shape))])
    return factor_of


def gaussian(stream_key, shape, scale, reach, cuts=(), dtype=jnp.bfloat16):
    drawn = jax.random.normal(stream_key, shape, jnp.float32) * scale
    if len(cuts) > 0:
        drawn = shard_levels(stream_key, shape, cuts, -0.22, 0.18) * drawn
    return jnp.clip(drawn, min=-reach, max=reach).astype(dtype)


def heavy_noise(stream_key, extent, scale, most, pieces, heavy, kind=jnp.bfloat16):
    result = scale * jax.random.normal(stream_key, extent, jnp.float32)
    if pieces:
        result = result * shard_levels(stream_key, extent, pieces, -0.22, 0.18)
    return jnp.clip(spiked(result, jax.random.fold_in(stream_key, 3), *heavy), -most, most).astype(kind)


def setup_inputs(seed: int = 0) -> dict:
    key_of = jax.random.split(jax.random.key(seed), 6)
    permittivity = jnp.clip(jnp.exp(math.log(2.0) - 0.6931472 * jax.random.uniform(key_of[0], (NX, NY, NZ), jnp.float32) ** shard_levels(key_of[0], (NX, NY, NZ), ((0, 32),), -0.2, 0.2)), 1.0, 2.0)
    e_start = gaussian(key_of[1], (SOURCES, 3, NX, NY, NZ), 1.0, 6.0, ((0, 8), (2, 4)), jnp.float32)
    h_start = gaussian(key_of[2], (SOURCES, 3, NX, NY, NZ), 1.0, 6.0, ((0, 8), (2, 4)), jnp.float32)
    e_cotangent = heavy_noise(key_of[3], (SOURCES, 3, NX, NY, NZ), 1.0, 6.0, ((0, 8), (2, 4)), (0, 2, 8, 2.0), jnp.float32)
    h_cotangent = gaussian(key_of[4], (SOURCES, 3, NX, NY, NZ), 1.0, 6.0, ((0, 8), (2, 4)), jnp.float32)
    return dict(permittivity=permittivity, e_start=e_start, h_start=h_start, e_cotangent=e_cotangent, h_cotangent=h_cotangent)


courant = 0.57

def ahead(field, axis):
    size = field.shape[axis]
    upper = lax.slice_in_dim(field, 1, size, axis=axis)
    zeros = jnp.zeros_like(lax.slice_in_dim(field, 0, 1, axis=axis))
    return jnp.concatenate([upper, zeros], axis) - field

def behind(field, axis):
    size = field.shape[axis]
    lower = lax.slice_in_dim(field, 0, size - 1, axis=axis)
    zeros = jnp.zeros_like(lax.slice_in_dim(field, 0, 1, axis=axis))
    return field - jnp.concatenate([zeros, lower], axis)

def curl_with(field, differ):
    return jnp.stack([differ(field[2], 1) - differ(field[1], 2), differ(field[0], 2) - differ(field[2], 0), differ(field[1], 0) - differ(field[0], 1)])

def leapfrog(inverse, efield, hfield):
    for turn in range(STEPS):
        hfield = hfield - courant * curl_with(efield, ahead)
        efield = efield + courant * inverse * curl_with(hfield, behind)
    return (efield, hfield)

def reference(permittivity, e_start, h_start, e_cotangent, h_cotangent):

    def per_source(total, items):
        efield, hfield, e_cot, h_cot = items
        outputs, pullback = jax.vjp(lambda perm: leapfrog(1.0 / perm, efield, hfield), permittivity)
        grad_perm, = pullback((e_cot, h_cot))
        return (total + grad_perm, outputs[0])
    start = jnp.zeros(permittivity.shape, jnp.float32)
    gradient, e_final = lax.scan(per_source, start, (e_start, h_start, e_cotangent, h_cotangent))
    return (e_final, gradient)
```

```python
import functools

import jax
import jax.numpy as jnp
from jax import lax
from jax.experimental import pallas as pl
from jax.experimental.pallas import tpu as pltpu
from jax.sharding import PartitionSpec as P

STEPS = 6
COURANT = 0.57
LANES = 128
ROWS = 8
MESH = pl.DeviceIdType.MESH


def group_of(total, most):
    return max(g for g in range(1, most + 1) if total % g == 0)


def over_planes(first, total, most, load, finish):
    group = group_of(total, most)

    def body(i, carry):
        base = first + i * group
        held = [load(base + j) for j in range(group)]
        for j in range(group):
            finish(base + j, held[j])
        return carry

    lax.fori_loop(0, total // group, body, 0)


def ahead_y(x):
    ny = x.shape[0]
    r = pltpu.roll(x, ny - 1, 0)
    low = r[ny - ROWS :]
    row = lax.broadcasted_iota(jnp.int32, low.shape, 0)
    low = jnp.where(row == ROWS - 1, 0.0, low)
    return jnp.concatenate([r[: ny - ROWS], low], 0) if ny > ROWS else low


def behind_y(x):
    ny = x.shape[0]
    r = pltpu.roll(x, 1, 0)
    top = r[:ROWS]
    row = lax.broadcasted_iota(jnp.int32, top.shape, 0)
    top = jnp.where(row == 0, 0.0, top)
    return jnp.concatenate([top, r[ROWS:]], 0) if ny > ROWS else top


def ahead_z(x):
    return pltpu.roll(x, x.shape[1] - 1, 1)


def behind_z(x):
    r = pltpu.roll(x, 1, 1)
    first = r[:, :LANES]
    lane = lax.broadcasted_iota(jnp.int32, first.shape, 1)
    first = jnp.where(lane == 0, 0.0, first)
    return jnp.concatenate([first, r[:, LANES:]], 1) if x.shape[1] > LANES else first


def kernel(
    tiles, sources,
    perm_ref, e_ref, h_ref, a_ref, b_ref,
    eout_ref, grad_ref,
    perm_in, e_in, h_in, a_in, b_in, e_last,
    coef, efield, hfield, ufield, bfield, deltas, grad, parts,
    in_sem, out_sem, perm_send, perm_recv, grad_send, grad_recv, halo_send, halo_recv,
):
    count, ny, nz = perm_in.shape
    wide = coef.shape[2]
    whole = nz // LANES * LANES
    rows = perm_ref.shape[0]
    tile = lax.axis_index("tile")
    me = lax.axis_index("src")
    has_below = tile > 0
    has_above = tile < tiles - 1
    own = pl.ds(me * rows, rows)

    loads = [
        pltpu.make_async_copy(e_ref.at[0], e_in, in_sem.at[0]),
        pltpu.make_async_copy(h_ref.at[0], h_in, in_sem.at[1]),
        pltpu.make_async_copy(perm_ref, perm_in.at[own], in_sem.at[2]),
        pltpu.make_async_copy(a_ref.at[0], a_in, in_sem.at[3]),
        pltpu.make_async_copy(b_ref.at[0], b_in, in_sem.at[4]),
    ]
    for copy in loads:
        copy.start()

    nothing = jnp.zeros((ny, wide), jnp.float32)
    for c in range(3):
        efield[c, count] = nothing
        hfield[c, 0] = nothing
        bfield[c, 0] = nothing
        for t in range(STEPS):
            ufield[t, c, count] = nothing

    barrier = pltpu.get_barrier_semaphore()
    for d in range(1, sources):
        pl.semaphore_signal(
            barrier, 1, device_id={"tile": tile, "src": lax.rem(me + d, sources)}, device_id_type=MESH
        )

    @pl.when(has_below)
    def _():
        pl.semaphore_signal(barrier, 1, device_id={"tile": tile - 1, "src": me}, device_id_type=MESH)

    @pl.when(has_above)
    def _():
        pl.semaphore_signal(barrier, 1, device_id={"tile": tile + 1, "src": me}, device_id_type=MESH)

    ends = jnp.where(has_below, 1, 0) + jnp.where(has_above, 1, 0)
    pl.semaphore_wait(barrier, sources - 1 + ends)

    def perm_copy(d):
        return pltpu.make_async_remote_copy(
            src_ref=perm_ref,
            dst_ref=perm_in.at[own],
            send_sem=perm_send.at[d - 1],
            recv_sem=perm_recv.at[d - 1],
            device_id={"tile": tile, "src": lax.rem(me + d, sources)},
            device_id_type=MESH,
        )

    def pad(ref, index, value):
        if whole:
            ref[index + (slice(None), slice(0, whole))] = value[:, :whole]
        if whole < nz:
            ref[index + (slice(None), slice(whole, nz))] = value[:, whole:]
        if nz < wide:
            ref[index + (slice(None), slice(nz, wide))] = jnp.zeros((ny, wide - nz), jnp.float32)

    def down(ref, slot):
        return pltpu.make_async_remote_copy(
            src_ref=ref.at[pl.ds(1, 2), 0],
            dst_ref=ref.at[pl.ds(1, 2), count],
            send_sem=halo_send.at[slot],
            recv_sem=halo_recv.at[slot],
            device_id={"tile": tile - 1, "src": me},
            device_id_type=MESH,
        )

    def up(ref, slot):
        return pltpu.make_async_remote_copy(
            src_ref=ref.at[pl.ds(1, 2), count],
            dst_ref=ref.at[pl.ds(1, 2), 0],
            send_sem=halo_send.at[slot],
            recv_sem=halo_recv.at[slot],
            device_id={"tile": tile + 1, "src": me},
            device_id_type=MESH,
        )

    def send_down(ref, slot):
        @pl.when(has_below)
        def _():
            down(ref, slot).start()

    def sent_down(ref, slot):
        @pl.when(has_below)
        def _():
            down(ref, slot).wait_send()

    def got_down(ref, slot):
        @pl.when(has_above)
        def _():
            down(ref, slot).wait_recv()

    def send_up(ref, slot):
        @pl.when(has_above)
        def _():
            up(ref, slot).start()

    def sent_up(ref, slot):
        @pl.when(has_above)
        def _():
            up(ref, slot).wait_send()

    def got_up(ref, slot):
        @pl.when(has_below)
        def _():
            up(ref, slot).wait_recv()

    def new_h(es, hs):
        def run(p):
            e0, e1, e2 = es[0, p], es[1, p], es[2, p]
            n1, n2 = es[1, p + 1], es[2, p + 1]
            h0 = hs[0, p + 1] - ((ahead_y(e2) - e2) - (ahead_z(e1) - e1))
            h1 = hs[1, p + 1] - ((ahead_z(e0) - e0) - (n2 - e2))
            h2 = hs[2, p + 1] - ((n1 - e1) - (ahead_y(e0) - e0))
            return h0, h1, h2

        return run

    def put_h(hs):
        def run(p, new):
            for c in range(3):
                hs[c, p + 1] = new[c]

        return run

    def new_e(es, hs):
        def run(p):
            h0, h1, h2 = hs[0, p + 1], hs[1, p + 1], hs[2, p + 1]
            m1, m2 = hs[1, p], hs[2, p]
            k = coef[p]
            d0 = k * ((h2 - behind_y(h2)) - (h1 - behind_z(h1)))
            d1 = k * ((h0 - behind_z(h0)) - (h2 - m2))
            d2 = k * ((h1 - m1) - (h0 - behind_y(h0)))
            d = (d0, d1, d2)
            return d, tuple(es[c, p] + d[c] for c in range(3))

        return run

    half = STEPS // 2

    def dot(left, right, p):
        return left[0] * right[0, p] + left[1] * right[1, p] + left[2] * right[2, p]

    def put_forward(t):
        def run(p, new):
            d, e = new
            if t == STEPS:
                for c in range(3):
                    e_last[c, p] = e[c][:, :nz]
            else:
                for c in range(3):
                    efield[c, p] = e[c]
            if t <= half:
                for c in range(3):
                    deltas[t, c, p] = d[c]
            else:
                grad[p] += dot(d, ufield.at[STEPS - t], p)

        return run

    def put_adjoint(t):
        def run(p, new):
            _, u = new
            if t < STEPS - 1:
                for c in range(3):
                    ufield[t, c, p] = u[c]
            if t >= half:
                term = dot(u, deltas.at[STEPS - t], p)
                grad[p] = term if t == half else grad[p] + term

        return run

    MOST = 5

    def h_inner(es, hs):
        over_planes(0, count - 1, MOST, new_h(es, hs), put_h(hs))

    def h_edge(es, hs):
        put_h(hs)(count - 1, new_h(es, hs)(count - 1))

    def e_inner(es, hs, put):
        over_planes(1, count - 1, MOST, new_e(es, hs), put)

    def e_edge(es, hs, put):
        put(0, new_e(es, hs)(0))

    loads[0].wait()

    def prepare_e(p):
        return tuple(e_in[c, p] for c in range(3))

    def finish_e(p, planes):
        for c in range(3):
            pad(efield, (c, p), planes[c])

    over_planes(0, count, 2, prepare_e, finish_e)
    send_down(efield, 0)
    for d in range(1, sources):
        perm_copy(d).start()
    loads[1].wait()

    def prepare_h(p):
        return tuple(h_in[c, p] * (1.0 / COURANT) for c in range(3))

    def finish_h(p, planes):
        for c in range(3):
            pad(hfield, (c, p + 1), planes[c])

    over_planes(0, count, 2, prepare_h, finish_h)
    h_inner(efield, hfield)
    got_down(efield, 0)
    h_edge(efield, hfield)
    send_up(hfield, 1)

    loads[4].wait()

    def prepare_b(p):
        return tuple(b_in[c, p] * (-1.0 / COURANT) for c in range(3))

    def finish_b(p, planes):
        for c in range(3):
            pad(bfield, (c, p + 1), planes[c])

    over_planes(0, count, 2, prepare_b, finish_b)
    loads[2].wait()
    loads[3].wait()
    for d in range(1, sources):
        perm_copy(d).wait_recv()

    def prepare_u(p):
        inverse = 1.0 / perm_in[p]
        return inverse * (COURANT * COURANT), tuple(inverse * a_in[c, p] for c in range(3))

    def finish_u(p, planes):
        k, u = planes
        pad(coef, (p,), k)
        for c in range(3):
            pad(ufield, (0, c, p), u[c])

    over_planes(0, count, 2, prepare_u, finish_u)
    send_down(ufield.at[0], 2)

    def grad_copy(d):
        peer = lax.rem(me + d, sources)
        return pltpu.make_async_remote_copy(
            src_ref=grad.at[pl.ds(peer * rows, rows)],
            dst_ref=parts.at[d - 1],
            send_sem=grad_send.at[d - 1],
            recv_sem=grad_recv.at[d - 1],
            device_id={"tile": tile, "src": peer},
            device_id_type=MESH,
        )

    for t in range(1, STEPS + 1):
        forward, adjoint = put_forward(t), put_adjoint(t)
        e_inner(efield, hfield, forward)
        if t < STEPS:
            h_inner(ufield.at[t - 1], bfield)
        else:
            for d in range(1, sources):
                @pl.when(lax.rem(me + d, sources) != 0)
                def _():
                    grad_copy(d).start()

            pltpu.make_async_copy(
                e_last.at[:, pl.ds(1, count - 1)], eout_ref.at[0, :, pl.ds(1, count - 1)], out_sem.at[0]
            ).start()
        got_up(hfield, 1)
        sent_down(efield, 0)
        e_edge(efield, hfield, forward)
        if t < STEPS:
            send_down(efield, 0)
            got_down(ufield.at[t - 1], 2)
            if t > 1:
                sent_up(bfield, 3)
            h_edge(ufield.at[t - 1], bfield)
            send_up(bfield, 3)
            sent_up(hfield, 1)
            h_inner(efield, hfield)
            e_inner(ufield.at[t - 1], bfield, adjoint) if t < STEPS else None
            got_down(efield, 0)
            h_edge(efield, hfield)
            send_up(hfield, 1)
            got_up(bfield, 3)
            e_edge(ufield.at[t - 1], bfield, adjoint)
            sent_down(ufield.at[t - 1], 2)
            if t < STEPS - 1:
                send_down(ufield.at[t], 2)

    for d in range(1, sources):
        @pl.when(lax.rem(me + d, sources) == 0)
        def _():
            grad_copy(d).start()

    tail = pltpu.make_async_copy(
        e_last.at[:, pl.ds(0, 1)], eout_ref.at[0, :, pl.ds(0, 1)], out_sem.at[1]
    )
    tail.start()
    sent_up(hfield, 1)
    sent_up(bfield, 3)
    total = grad[own]
    for d in range(1, sources):
        grad_copy(d).wait_recv()
        total = total + parts[d - 1]
    grad_ref[...] = -total[:, :, :nz]
    for d in range(1, sources):
        perm_copy(d).wait_send()
        grad_copy(d).wait_send()
    pltpu.make_async_copy(
        e_last.at[:, pl.ds(1, count - 1)], eout_ref.at[0, :, pl.ds(1, count - 1)], out_sem.at[0]
    ).wait()
    tail.wait()


def on_device(tiles, sources, permittivity, e_start, h_start, e_cotangent, h_cotangent):
    rows, ny, nz = permittivity.shape
    count = rows * sources
    wide = -(-nz // LANES) * LANES
    any_spec = pl.BlockSpec(memory_space=pl.ANY)
    vmem = lambda *shape: pltpu.VMEM(shape, jnp.float32)
    dma = lambda n: pltpu.SemaphoreType.DMA((n,))
    return pl.pallas_call(
        functools.partial(kernel, tiles, sources),
        out_shape=(
            jax.ShapeDtypeStruct(e_start.shape, jnp.float32),
            jax.ShapeDtypeStruct(permittivity.shape, jnp.float32),
        ),
        in_specs=[any_spec] * 5,
        out_specs=(any_spec, pl.BlockSpec(memory_space=pltpu.VMEM)),
        scratch_shapes=[
            vmem(count, ny, nz),
            vmem(3, count, ny, nz),
            vmem(3, count, ny, nz),
            vmem(3, count, ny, nz),
            vmem(3, count, ny, nz),
            vmem(3, count, ny, nz),
            vmem(count, ny, wide),
            vmem(3, count + 1, ny, wide),
            vmem(3, count + 1, ny, wide),
            vmem(STEPS, 3, count + 1, ny, wide),
            vmem(3, count + 1, ny, wide),
            vmem(STEPS // 2 + 1, 3, count, ny, wide),
            vmem(count, ny, wide),
            vmem(sources - 1, rows, ny, wide),
            dma(5),
            dma(2),
            dma(sources - 1),
            dma(sources - 1),
            dma(sources - 1),
            dma(sources - 1),
            dma(4),
            dma(4),
        ],
        compiler_params=pltpu.CompilerParams(
            collective_id=0, has_side_effects=True, vmem_limit_bytes=48 * 1024 * 1024
        ),
    )(permittivity, e_start, h_start, e_cotangent, h_cotangent)


def solution(mesh):
    fields = P("src", None, "tile", None, None)
    cells = P(("tile", "src"), None, None)
    return jax.shard_map(
        functools.partial(on_device, mesh.shape["tile"], mesh.shape["src"]),
        mesh=mesh,
        in_specs=(cells, fields, fields, fields, fields),
        out_specs=(fields, cells),
        check_vma=False,
    )
```

```python
import functools

import jax
import jax.numpy as jnp
from jax import lax
from jax.experimental import pallas as pl
from jax.experimental.pallas import tpu as pltpu
from jax.sharding import PartitionSpec as P

STEPS = 6
COURANT = 0.57
LANES = 128
ROWS = 8
MESH = pl.DeviceIdType.MESH


def group_of(total, most):
    return max(g for g in range(1, most + 1) if total % g == 0)


def over_planes(first, total, most, run):
    group = group_of(total, most)

    def body(i, carry):
        run(first + i * group, group)
        return carry

    lax.fori_loop(0, total // group, body, 0)


def ahead_y(x):
    ny = x.shape[0]
    r = pltpu.roll(x, ny - 1, 0)
    low = r[ny - ROWS :]
    row = lax.broadcasted_iota(jnp.int32, low.shape, 0)
    low = jnp.where(row == ROWS - 1, 0.0, low)
    return jnp.concatenate([r[: ny - ROWS], low], 0) if ny > ROWS else low


def behind_y(x):
    ny = x.shape[0]
    r = pltpu.roll(x, 1, 0)
    top = r[:ROWS]
    row = lax.broadcasted_iota(jnp.int32, top.shape, 0)
    top = jnp.where(row == 0, 0.0, top)
    return jnp.concatenate([top, r[ROWS:]], 0) if ny > ROWS else top


def ahead_z(x):
    return pltpu.roll(x, x.shape[1] - 1, 1)


def behind_z(x):
    r = pltpu.roll(x, 1, 1)
    first = r[:, :LANES]
    lane = lax.broadcasted_iota(jnp.int32, first.shape, 1)
    first = jnp.where(lane == 0, 0.0, first)
    return jnp.concatenate([first, r[:, LANES:]], 1) if x.shape[1] > LANES else first


def kernel(
    tiles, sources,
    perm_ref, e_ref, h_ref, a_ref, b_ref,
    eout_ref, grad_ref,
    perm_in, e_in, h_in, a_in, b_in, e_last,
    coef, efield, hfield, ufield, bfield, halos, deltas, grad, parts,
    in_sem, out_sem, perm_send, perm_recv, grad_send, grad_recv, halo_send, halo_recv,
):
    count, ny, nz = perm_in.shape
    wide = coef.shape[2]
    whole = nz // LANES * LANES
    rows = perm_ref.shape[0]
    tile = lax.axis_index("tile")
    me = lax.axis_index("src")
    has_below = tile > 0
    has_above = tile < tiles - 1
    own = pl.ds(me * rows, rows)

    loads = [
        pltpu.make_async_copy(e_ref.at[0], e_in, in_sem.at[0]),
        pltpu.make_async_copy(h_ref.at[0], h_in, in_sem.at[1]),
        pltpu.make_async_copy(perm_ref, perm_in.at[own], in_sem.at[2]),
        pltpu.make_async_copy(a_ref.at[0], a_in, in_sem.at[3]),
        pltpu.make_async_copy(b_ref.at[0], b_in, in_sem.at[4]),
    ]
    for copy in loads:
        copy.start()

    nothing = jnp.zeros((ny, wide), jnp.float32)
    for c in range(3):
        efield[c, count] = nothing
        hfield[c, 0] = nothing
        bfield[c, 0] = nothing
        for t in range(STEPS):
            ufield[t, c, count] = nothing

    barrier = pltpu.get_barrier_semaphore()
    for d in range(1, sources):
        pl.semaphore_signal(
            barrier, 1, device_id={"tile": tile, "src": lax.rem(me + d, sources)}, device_id_type=MESH
        )

    @pl.when(has_below)
    def _():
        pl.semaphore_signal(barrier, 1, device_id={"tile": tile - 1, "src": me}, device_id_type=MESH)

    @pl.when(has_above)
    def _():
        pl.semaphore_signal(barrier, 1, device_id={"tile": tile + 1, "src": me}, device_id_type=MESH)

    ends = jnp.where(has_below, 1, 0) + jnp.where(has_above, 1, 0)
    pl.semaphore_wait(barrier, sources - 1 + ends)

    def perm_copy(d):
        return pltpu.make_async_remote_copy(
            src_ref=perm_ref,
            dst_ref=perm_in.at[own],
            send_sem=perm_send.at[d - 1],
            recv_sem=perm_recv.at[d - 1],
            device_id={"tile": tile, "src": lax.rem(me + d, sources)},
            device_id_type=MESH,
        )

    for d in range(1, sources):
        perm_copy(d).start()

    def pad(ref, index, value):
        if whole:
            ref[index + (slice(None), slice(0, whole))] = value[:, :whole]
        if whole < nz:
            ref[index + (slice(None), slice(whole, nz))] = value[:, whole:]
        if nz < wide:
            ref[index + (slice(None), slice(nz, wide))] = jnp.zeros((ny, wide - nz), jnp.float32)

    def down(ref, slot, c):
        return pltpu.make_async_remote_copy(
            src_ref=ref.at[c, 0],
            dst_ref=halos.at[slot, c - 1],
            send_sem=halo_send.at[slot, c - 1],
            recv_sem=halo_recv.at[slot, c - 1],
            device_id={"tile": tile - 1, "src": me},
            device_id_type=MESH,
        )

    def up(ref, slot, c):
        return pltpu.make_async_remote_copy(
            src_ref=ref.at[c, count],
            dst_ref=halos.at[slot, c - 1],
            send_sem=halo_send.at[slot, c - 1],
            recv_sem=halo_recv.at[slot, c - 1],
            device_id={"tile": tile + 1, "src": me},
            device_id_type=MESH,
        )

    def send_down(ref, slot, c):
        @pl.when(has_below)
        def _():
            down(ref, slot, c).start()

    def send_up(ref, slot, c):
        @pl.when(has_above)
        def _():
            up(ref, slot, c).start()

    def sent_down(ref, slot):
        @pl.when(has_below)
        def _():
            for c in (2, 1):
                down(ref, slot, c).wait_send()

    def sent_up(ref, slot):
        @pl.when(has_above)
        def _():
            for c in (1, 2):
                up(ref, slot, c).wait_send()

    def step_h(es, hs):
        def run(base, group):
            e0, e1, e2 = es[0, base], es[1, base], es[2, base]
            for j in range(group):
                p = base + j
                n1, n2 = es[1, p + 1], es[2, p + 1]
                hs[0, p + 1] -= (ahead_y(e2) - e2) - (ahead_z(e1) - e1)
                hs[1, p + 1] -= (ahead_z(e0) - e0) - (n2 - e2)
                hs[2, p + 1] -= (n1 - e1) - (ahead_y(e0) - e0)
                e1, e2 = n1, n2
                if j < group - 1:
                    e0 = es[0, p + 1]

        over_planes(0, count, MOST, run)

    def edge_h(es, hs, slot_in, slot_out):
        for c, other, sign in ((1, 2, 1.0), (2, 1, -1.0)):
            @pl.when(has_above)
            def _():
                down(es, slot_in, other).wait_recv()
                hs[c, count] += sign * halos[slot_in, other - 1]

            send_up(hs, slot_out, c)

    def step_e(hs, put):
        def run(base, group):
            m1, m2 = hs[1, base], hs[2, base]
            for p in [base + j for j in range(group)]:
                h0, h1, h2 = hs[0, p + 1], hs[1, p + 1], hs[2, p + 1]
                k = coef[p]
                put(
                    p,
                    (
                        k * ((h2 - behind_y(h2)) - (h1 - behind_z(h1))),
                        k * ((h0 - behind_z(h0)) - (h2 - m2)),
                        k * ((h1 - m1) - (h0 - behind_y(h0))),
                    ),
                )
                m1, m2 = h1, h2

        over_planes(0, count, MOST, run)

    def edge_e(hs, slot_in, fix, send):
        for c, other, sign in ((2, 1, -1.0), (1, 2, 1.0)):
            @pl.when(has_below)
            def _():
                up(hs, slot_in, other).wait_recv()
                fix(c, sign * (coef[0] * halos[slot_in, other - 1]))

            send(c)

    half = STEPS // 2

    def dot(left, right, p):
        return left[0] * right[0, p] + left[1] * right[1, p] + left[2] * right[2, p]

    def forward(t):
        def put(p, d):
            for c in range(3):
                if t == STEPS:
                    e_last[c, p] = (efield[c, p] + d[c])[:, :nz]
                else:
                    efield[c, p] += d[c]
                if t <= half:
                    deltas[t, c, p] = d[c]
            if t > half:
                grad[p] += dot(d, ufield.at[STEPS - t], p)

        def fix(c, d):
            if t == STEPS:
                e_last[c, 0] += d[:, :nz]
            else:
                efield[c, 0] += d
            if t <= half:
                deltas[t, c, 0] += d
            else:
                grad[0] += d * ufield[STEPS - t, c, 0]

        return put, fix

    def adjoint(t):
        def put(p, d):
            u = tuple(ufield[t - 1, c, p] + d[c] for c in range(3))
            if t < STEPS - 1:
                for c in range(3):
                    ufield[t, c, p] = u[c]
            if t >= half:
                term = dot(u, deltas.at[STEPS - t], p)
                grad[p] = term if t == half else grad[p] + term

        def fix(c, d):
            if t < STEPS - 1:
                ufield[t, c, 0] += d
            if t >= half:
                grad[0] += d * deltas[STEPS - t, c, 0]

        return put, fix

    MOST = 4

    loads[0].wait()

    def prepare_e(base, group):
        for p in [base + j for j in range(group)]:
            for c in range(3):
                pad(efield, (c, p), e_in[c, p])

    prepare_e(0, 1)
    for c in (2, 1):
        send_down(efield, 0, c)
    over_planes(1, count - 1, 3, prepare_e)
    loads[1].wait()

    def prepare_h(base, group):
        for p in [base + j for j in range(group)]:
            for c in range(3):
                pad(hfield, (c, p + 1), h_in[c, p] * (1.0 / COURANT))

    over_planes(0, count, 2, prepare_h)
    step_h(efield, hfield)
    edge_h(efield, hfield, 0, 1)

    loads[4].wait()

    def prepare_b(base, group):
        for p in [base + j for j in range(group)]:
            for c in range(3):
                pad(bfield, (c, p + 1), b_in[c, p] * (-1.0 / COURANT))

    over_planes(0, count, 2, prepare_b)
    loads[2].wait()
    loads[3].wait()
    for d in range(1, sources):
        perm_copy(d).wait_recv()

    def prepare_u(base, group):
        for p in [base + j for j in range(group)]:
            inverse = 1.0 / perm_in[p]
            pad(coef, (p,), inverse * (COURANT * COURANT))
            for c in range(3):
                pad(ufield, (0, c, p), inverse * a_in[c, p])

    prepare_u(0, 1)
    for c in (2, 1):
        send_down(ufield.at[0], 2, c)
    over_planes(1, count - 1, 3, prepare_u)

    def grad_copy(d):
        peer = lax.rem(me + d, sources)
        return pltpu.make_async_remote_copy(
            src_ref=grad.at[pl.ds(peer * rows, rows)],
            dst_ref=parts.at[d - 1],
            send_sem=grad_send.at[d - 1],
            recv_sem=grad_recv.at[d - 1],
            device_id={"tile": tile, "src": peer},
            device_id_type=MESH,
        )

    for t in range(1, STEPS + 1):
        last = t == STEPS
        before = ufield.at[t - 1]
        put, fix = forward(t)
        sent_down(efield, 0)
        step_e(hfield, put)
        if not last:
            if t > 1:
                sent_up(bfield, 3)
            step_h(before, bfield)
        else:
            for d in range(1, sources):
                @pl.when(lax.rem(me + d, sources) != 0)
                def _():
                    grad_copy(d).start()

            pltpu.make_async_copy(
                e_last.at[:, pl.ds(1, count - 1)], eout_ref.at[0, :, pl.ds(1, count - 1)], out_sem.at[0]
            ).start()
        edge_e(hfield, 1, fix, lambda c: None if last else send_down(efield, 0, c))
        if last:
            break
        edge_h(before, bfield, 2, 3)
        put, fix = adjoint(t)
        sent_up(hfield, 1)
        step_h(efield, hfield)
        sent_down(before, 2)
        step_e(bfield, put)
        edge_h(efield, hfield, 0, 1)
        edge_e(bfield, 3, fix, lambda c: send_down(ufield.at[t], 2, c) if t < STEPS - 1 else None)

    for d in range(1, sources):
        @pl.when(lax.rem(me + d, sources) == 0)
        def _():
            grad_copy(d).start()

    tail = pltpu.make_async_copy(
        e_last.at[:, pl.ds(0, 1)], eout_ref.at[0, :, pl.ds(0, 1)], out_sem.at[1]
    )
    tail.start()
    sent_up(hfield, 1)
    sent_up(bfield, 3)
    total = grad[own]
    for d in range(1, sources):
        grad_copy(d).wait_recv()
        total = total + parts[d - 1]
    grad_ref[...] = -total[:, :, :nz]
    for d in range(1, sources):
        perm_copy(d).wait_send()
        grad_copy(d).wait_send()
    pltpu.make_async_copy(
        e_last.at[:, pl.ds(1, count - 1)], eout_ref.at[0, :, pl.ds(1, count - 1)], out_sem.at[0]
    ).wait()
    tail.wait()


def on_device(tiles, sources, permittivity, e_start, h_start, e_cotangent, h_cotangent):
    rows, ny, nz = permittivity.shape
    count = rows * sources
    wide = -(-nz // LANES) * LANES
    any_spec = pl.BlockSpec(memory_space=pltpu.HBM)
    vmem = lambda *shape: pltpu.VMEM(shape, jnp.float32)
    dma = lambda n: pltpu.SemaphoreType.DMA((n,))
    return pl.pallas_call(
        functools.partial(kernel, tiles, sources),
        out_shape=(
            jax.ShapeDtypeStruct(e_start.shape, jnp.float32),
            jax.ShapeDtypeStruct(permittivity.shape, jnp.float32),
        ),
        in_specs=[any_spec] * 5,
        out_specs=(any_spec, pl.BlockSpec(memory_space=pltpu.VMEM)),
        scratch_shapes=[
            vmem(count, ny, nz),
            vmem(3, count, ny, nz),
            vmem(3, count, ny, nz),
            vmem(3, count, ny, nz),
            vmem(3, count, ny, nz),
            vmem(3, count, ny, nz),
            vmem(count, ny, wide),
            vmem(3, count + 1, ny, wide),
            vmem(3, count + 1, ny, wide),
            vmem(STEPS, 3, count + 1, ny, wide),
            vmem(3, count + 1, ny, wide),
            vmem(4, 2, ny, wide),
            vmem(STEPS // 2 + 1, 3, count, ny, wide),
            vmem(count, ny, wide),
            vmem(sources - 1, rows, ny, wide),
            dma(5),
            dma(2),
            dma(sources - 1),
            dma(sources - 1),
            dma(sources - 1),
            dma(sources - 1),
            pltpu.SemaphoreType.DMA((4, 2)),
            pltpu.SemaphoreType.DMA((4, 2)),
        ],
        compiler_params=pltpu.CompilerParams(
            collective_id=0, has_side_effects=True, vmem_limit_bytes=60 * 1024 * 1024
        ),
    )(permittivity, e_start, h_start, e_cotangent, h_cotangent)


def solution(mesh):
    fields = P("src", None, "tile", None, None)
    cells = P(("tile", "src"), None, None)
    return jax.shard_map(
        functools.partial(on_device, mesh.shape["tile"], mesh.shape["src"]),
        mesh=mesh,
        in_specs=(cells, fields, fields, fields, fields),
        out_specs=(fields, cells),
        check_vma=False,
    )
```

```python
import functools

import jax
import jax.numpy as jnp
from jax import lax
from jax.experimental import pallas as pl
from jax.experimental.pallas import tpu as pltpu
from jax.sharding import PartitionSpec as P

STEPS = 6
COURANT = 0.57
LANES = 128
ROWS = 8
MESH = pl.DeviceIdType.MESH


def group_of(total, most):
    return max(g for g in range(1, most + 1) if total % g == 0)


def over_planes(first, total, most, run):
    group = group_of(total, most)

    def body(i, carry):
        run(first + i * group, group)
        return carry

    lax.fori_loop(0, total // group, body, 0)


def ahead_z(x):
    r = pltpu.roll(x, LANES - 1, 2)
    after = jnp.concatenate([r[1:], jnp.zeros_like(r[:1])], 0)
    lane = lax.broadcasted_iota(jnp.int32, r.shape, 2)
    return jnp.where(lane == LANES - 1, after, r)


def behind_z(x):
    r = pltpu.roll(x, 1, 2)
    before = jnp.concatenate([jnp.zeros_like(r[:1]), r[:-1]], 0)
    lane = lax.broadcasted_iota(jnp.int32, r.shape, 2)
    return jnp.where(lane == 0, before, r)


def kernel(
    tiles, sources,
    perm_ref, e_ref, h_ref, a_ref, b_ref,
    eout_ref, grad_ref,
    perm_in, e_in, h_in, a_in, b_in, e_last,
    coef, efield, hfield, ufield, bfield, halos, deltas, grad, parts,
    in_sem, out_sem, perm_send, perm_recv, grad_send, grad_recv, halo_send, halo_recv,
):
    count, ny, nz = perm_in.shape
    chunks = coef.shape[1]
    erows, hrows = pl.ds(0, ny), pl.ds(ROWS, ny)
    eahead, hbehind = pl.ds(1, ny), pl.ds(ROWS - 1, ny)
    rows = perm_ref.shape[0]
    tile = lax.axis_index("tile")
    me = lax.axis_index("src")
    has_below = tile > 0
    has_above = tile < tiles - 1
    own = pl.ds(me * rows, rows)

    loads = [
        pltpu.make_async_copy(e_ref.at[0], e_in, in_sem.at[0]),
        pltpu.make_async_copy(h_ref.at[0], h_in, in_sem.at[1]),
        pltpu.make_async_copy(perm_ref, perm_in.at[own], in_sem.at[2]),
        pltpu.make_async_copy(a_ref.at[0], a_in, in_sem.at[3]),
        pltpu.make_async_copy(b_ref.at[0], b_in, in_sem.at[4]),
    ]
    for copy in loads:
        copy.start()

    nothing = jnp.zeros((chunks, ny, LANES), jnp.float32)
    for c in (1, 2):
        efield[c, count, :, erows] = nothing
        hfield[c, 0, :, hrows] = nothing
        bfield[c, 0, :, hrows] = nothing
        for t in range(STEPS - 1):
            ufield[t, c, count, :, erows] = nothing

    def clear(p, carry):
        margin = jnp.zeros((chunks, ROWS, LANES), jnp.float32)
        for c in (0, 2):
            efield[c, p, :, pl.ds(ny, ROWS)] = margin
            hfield[c, p + 1, :, pl.ds(0, ROWS)] = margin
            bfield[c, p + 1, :, pl.ds(0, ROWS)] = margin
            for t in range(STEPS - 1):
                ufield[t, c, p, :, pl.ds(ny, ROWS)] = margin
        return carry

    lax.fori_loop(0, count, clear, 0)

    barrier = pltpu.get_barrier_semaphore()
    for d in range(1, sources):
        pl.semaphore_signal(
            barrier, 1, device_id={"tile": tile, "src": lax.rem(me + d, sources)}, device_id_type=MESH
        )

    @pl.when(has_below)
    def _():
        pl.semaphore_signal(barrier, 1, device_id={"tile": tile - 1, "src": me}, device_id_type=MESH)

    @pl.when(has_above)
    def _():
        pl.semaphore_signal(barrier, 1, device_id={"tile": tile + 1, "src": me}, device_id_type=MESH)

    ends = jnp.where(has_below, 1, 0) + jnp.where(has_above, 1, 0)
    pl.semaphore_wait(barrier, sources - 1 + ends)

    def perm_copy(d):
        return pltpu.make_async_remote_copy(
            src_ref=perm_ref,
            dst_ref=perm_in.at[own],
            send_sem=perm_send.at[d - 1],
            recv_sem=perm_recv.at[d - 1],
            device_id={"tile": tile, "src": lax.rem(me + d, sources)},
            device_id_type=MESH,
        )

    for d in range(1, sources):
        perm_copy(d).start()

    def pad(ref, index, start, value):
        for j in range(chunks):
            part = value[:, j * LANES : (j + 1) * LANES]
            have = part.shape[1]
            at = index + (j, pl.ds(start, ny))
            if have == LANES:
                ref[at] = part
            else:
                ref[at + (pl.ds(0, have),)] = part
                ref[at + (pl.ds(have, LANES - have),)] = jnp.zeros((ny, LANES - have), jnp.float32)

    def unpad(value, j):
        return value[..., : min(LANES, nz - j * LANES)]

    def down(ref, slot, c):
        return pltpu.make_async_remote_copy(
            src_ref=ref.at[c, 0, :, erows],
            dst_ref=halos.at[slot, c - 1],
            send_sem=halo_send.at[slot, c - 1],
            recv_sem=halo_recv.at[slot, c - 1],
            device_id={"tile": tile - 1, "src": me},
            device_id_type=MESH,
        )

    def up(ref, slot, c):
        return pltpu.make_async_remote_copy(
            src_ref=ref.at[c, count, :, hrows],
            dst_ref=halos.at[slot, c - 1],
            send_sem=halo_send.at[slot, c - 1],
            recv_sem=halo_recv.at[slot, c - 1],
            device_id={"tile": tile + 1, "src": me},
            device_id_type=MESH,
        )

    def send_down(ref, slot, c):
        @pl.when(has_below)
        def _():
            down(ref, slot, c).start()

    def send_up(ref, slot, c):
        @pl.when(has_above)
        def _():
            up(ref, slot, c).start()

    def sent_down(ref, slot):
        @pl.when(has_below)
        def _():
            for c in (2, 1):
                down(ref, slot, c).wait_send()

    def sent_up(ref, slot):
        @pl.when(has_above)
        def _():
            for c in (1, 2):
                up(ref, slot, c).wait_send()

    def step_h(es, hs):
        def run(base, group):
            e1, e2 = es[1, base, :, erows], es[2, base, :, erows]
            for j in range(group):
                p = base + j
                e0 = es[0, p, :, erows]
                n1, n2 = es[1, p + 1, :, erows], es[2, p + 1, :, erows]
                hs[0, p + 1, :, hrows] -= (es[2, p, :, eahead] - e2) - (ahead_z(e1) - e1)
                hs[1, p + 1, :, hrows] -= (ahead_z(e0) - e0) - (n2 - e2)
                hs[2, p + 1, :, hrows] -= (n1 - e1) - (es[0, p, :, eahead] - e0)
                e1, e2 = n1, n2

        over_planes(0, count, MOST, run)

    def edge_h(es, hs, slot_in, slot_out):
        for c, other, sign in ((1, 2, 1.0), (2, 1, -1.0)):
            @pl.when(has_above)
            def _():
                down(es, slot_in, other).wait_recv()
                hs[c, count, :, hrows] += sign * halos[slot_in, other - 1]

            send_up(hs, slot_out, c)

    def step_e(hs, put):
        def run(base, group):
            m1, m2 = hs[1, base, :, hrows], hs[2, base, :, hrows]
            for p in [base + j for j in range(group)]:
                h0, h1, h2 = (hs[c, p + 1, :, hrows] for c in range(3))
                k = coef[p]
                put(
                    p,
                    (
                        k * ((h2 - hs[2, p + 1, :, hbehind]) - (h1 - behind_z(h1))),
                        k * ((h0 - behind_z(h0)) - (h2 - m2)),
                        k * ((h1 - m1) - (h0 - hs[0, p + 1, :, hbehind])),
                    ),
                )
                m1, m2 = h1, h2

        over_planes(0, count, MOST, run)

    def edge_e(hs, slot_in, fix, send):
        for c, other, sign in ((2, 1, -1.0), (1, 2, 1.0)):
            @pl.when(has_below)
            def _():
                up(hs, slot_in, other).wait_recv()
                fix(c, sign * (coef[0] * halos[slot_in, other - 1]))

            send(c)

    half = STEPS // 2

    def dot(left, right):
        return left[0] * right[0] + left[1] * right[1] + left[2] * right[2]

    def put_last(c, p, value):
        for j in range(chunks):
            part = unpad(value[j], j)
            e_last[c, p, :, pl.ds(j * LANES, part.shape[1])] = part

    def forward(t):
        def put(p, d):
            for c in range(3):
                if t == STEPS:
                    put_last(c, p, efield[c, p, :, erows] + d[c])
                else:
                    efield[c, p, :, erows] += d[c]
                if t <= half:
                    deltas[t, c, p] = d[c]
            if t > half:
                grad[p] += dot(d, [ufield[STEPS - t, c, p, :, erows] for c in range(3)])

        def fix(c, d):
            if t == STEPS:
                for j in range(chunks):
                    part = unpad(d[j], j)
                    e_last[c, 0, :, pl.ds(j * LANES, part.shape[1])] += part
            else:
                efield[c, 0, :, erows] += d
            if t <= half:
                deltas[t, c, 0] += d
            else:
                grad[0] += d * ufield[STEPS - t, c, 0, :, erows]

        return put, fix

    def adjoint(t):
        def put(p, d):
            u = tuple(ufield[t - 1, c, p, :, erows] + d[c] for c in range(3))
            if t < STEPS - 1:
                for c in range(3):
                    ufield[t, c, p, :, erows] = u[c]
            if t >= half:
                term = dot(u, [deltas[STEPS - t, c, p] for c in range(3)])
                grad[p] = term if t == half else grad[p] + term

        def fix(c, d):
            if t < STEPS - 1:
                ufield[t, c, 0, :, erows] += d
            if t >= half:
                grad[0] += d * deltas[STEPS - t, c, 0]

        return put, fix

    MOST = 4

    loads[0].wait()

    def prepare_e(base, group):
        for p in [base + j for j in range(group)]:
            for c in range(3):
                pad(efield, (c, p), 0, e_in[c, p])

    prepare_e(0, 1)
    for c in (2, 1):
        send_down(efield, 0, c)
    over_planes(1, count - 1, 3, prepare_e)
    loads[1].wait()

    def prepare_h(base, group):
        for p in [base + j for j in range(group)]:
            for c in range(3):
                pad(hfield, (c, p + 1), ROWS, h_in[c, p] * (1.0 / COURANT))

    over_planes(0, count, 2, prepare_h)
    step_h(efield, hfield)
    edge_h(efield, hfield, 0, 1)

    loads[4].wait()

    def prepare_b(base, group):
        for p in [base + j for j in range(group)]:
            for c in range(3):
                pad(bfield, (c, p + 1), ROWS, b_in[c, p] * (-1.0 / COURANT))

    over_planes(0, count, 2, prepare_b)
    loads[2].wait()
    loads[3].wait()
    for d in range(1, sources):
        perm_copy(d).wait_recv()

    def prepare_u(base, group):
        for p in [base + j for j in range(group)]:
            inverse = 1.0 / perm_in[p]
            pad(coef, (p,), 0, inverse * (COURANT * COURANT))
            for c in range(3):
                pad(ufield, (0, c, p), 0, inverse * a_in[c, p])

    prepare_u(0, 1)
    for c in (2, 1):
        send_down(ufield.at[0], 2, c)
    over_planes(1, count - 1, 3, prepare_u)

    def grad_copy(d):
        peer = lax.rem(me + d, sources)
        return pltpu.make_async_remote_copy(
            src_ref=grad.at[pl.ds(peer * rows, rows)],
            dst_ref=parts.at[d - 1],
            send_sem=grad_send.at[d - 1],
            recv_sem=grad_recv.at[d - 1],
            device_id={"tile": tile, "src": peer},
            device_id_type=MESH,
        )

    for t in range(1, STEPS + 1):
        last = t == STEPS
        before = ufield.at[min(t, STEPS - 1) - 1]
        put, fix = forward(t)
        sent_down(efield, 0)
        step_e(hfield, put)
        if not last:
            if t > 1:
                sent_up(bfield, 3)
            step_h(before, bfield)
        else:
            for d in range(1, sources):
                @pl.when(lax.rem(me + d, sources) != 0)
                def _():
                    grad_copy(d).start()

            pltpu.make_async_copy(
                e_last.at[:, pl.ds(1, count - 1)], eout_ref.at[0, :, pl.ds(1, count - 1)], out_sem.at[0]
            ).start()
        edge_e(hfield, 1, fix, lambda c: None if last else send_down(efield, 0, c))
        if last:
            break
        edge_h(before, bfield, 2, 3)
        put, fix = adjoint(t)
        sent_up(hfield, 1)
        step_h(efield, hfield)
        sent_down(before, 2)
        step_e(bfield, put)
        edge_h(efield, hfield, 0, 1)
        edge_e(bfield, 3, fix, lambda c: send_down(ufield.at[t], 2, c) if t < STEPS - 1 else None)

    for d in range(1, sources):
        @pl.when(lax.rem(me + d, sources) == 0)
        def _():
            grad_copy(d).start()

    tail = pltpu.make_async_copy(
        e_last.at[:, pl.ds(0, 1)], eout_ref.at[0, :, pl.ds(0, 1)], out_sem.at[1]
    )
    tail.start()
    sent_up(hfield, 1)
    sent_up(bfield, 3)
    total = grad[own]
    for d in range(1, sources):
        grad_copy(d).wait_recv()
        total = total + parts[d - 1]
    for j in range(chunks):
        part = unpad(total[:, j], j)
        grad_ref[:, :, pl.ds(j * LANES, part.shape[2])] = -part
    for d in range(1, sources):
        perm_copy(d).wait_send()
        grad_copy(d).wait_send()
    pltpu.make_async_copy(
        e_last.at[:, pl.ds(1, count - 1)], eout_ref.at[0, :, pl.ds(1, count - 1)], out_sem.at[0]
    ).wait()
    tail.wait()


def on_device(tiles, sources, permittivity, e_start, h_start, e_cotangent, h_cotangent):
    rows, ny, nz = permittivity.shape
    count = rows * sources
    chunks = -(-nz // LANES)
    any_spec = pl.BlockSpec(memory_space=pltpu.HBM)
    vmem = lambda *shape: pltpu.VMEM(shape, jnp.float32)
    dma = lambda n: pltpu.SemaphoreType.DMA((n,))
    return pl.pallas_call(
        functools.partial(kernel, tiles, sources),
        out_shape=(
            jax.ShapeDtypeStruct(e_start.shape, jnp.float32),
            jax.ShapeDtypeStruct(permittivity.shape, jnp.float32),
        ),
        in_specs=[any_spec] * 5,
        out_specs=(any_spec, pl.BlockSpec(memory_space=pltpu.VMEM)),
        scratch_shapes=[
            vmem(count, ny, nz),
            vmem(3, count, ny, nz),
            vmem(3, count, ny, nz),
            vmem(3, count, ny, nz),
            vmem(3, count, ny, nz),
            vmem(3, count, ny, nz),
            vmem(count, chunks, ny, LANES),
            vmem(3, count + 1, chunks, ny + ROWS, LANES),
            vmem(3, count + 1, chunks, ny + ROWS, LANES),
            vmem(STEPS - 1, 3, count + 1, chunks, ny + ROWS, LANES),
            vmem(3, count + 1, chunks, ny + ROWS, LANES),
            vmem(4, 2, chunks, ny, LANES),
            vmem(STEPS // 2 + 1, 3, count, chunks, ny, LANES),
            vmem(count, chunks, ny, LANES),
            vmem(sources - 1, rows, chunks, ny, LANES),
            dma(5),
            dma(2),
            dma(sources - 1),
            dma(sources - 1),
            dma(sources - 1),
            dma(sources - 1),
            pltpu.SemaphoreType.DMA((4, 2)),
            pltpu.SemaphoreType.DMA((4, 2)),
        ],
        compiler_params=pltpu.CompilerParams(
            collective_id=0, has_side_effects=True, vmem_limit_bytes=60 * 1024 * 1024
        ),
    )(permittivity, e_start, h_start, e_cotangent, h_cotangent)


def solution(mesh):
    fields = P("src", None, "tile", None, None)
    cells = P(("tile", "src"), None, None)
    return jax.shard_map(
        functools.partial(on_device, mesh.shape["tile"], mesh.shape["src"]),
        mesh=mesh,
        in_specs=(cells, fields, fields, fields, fields),
        out_specs=(fields, cells),
        check_vma=False,
    )
```

```python
import functools

import jax
import jax.numpy as jnp
from jax import lax
from jax.experimental import pallas as pl
from jax.experimental.pallas import tpu as pltpu
from jax.sharding import PartitionSpec as P

STEPS = 6
COURANT = 0.57
LANES = 128
ROWS = 8
MESH = pl.DeviceIdType.MESH


def group_of(total, most):
    return max(g for g in range(1, most + 1) if total % g == 0)


def over_planes(first, total, most, run):
    group = group_of(total, most)

    def body(i, carry):
        run(first + i * group, group)
        return carry

    lax.fori_loop(0, total // group, body, 0)


def ahead_z(x):
    r = pltpu.roll(x, LANES - 1, 2)
    after = jnp.concatenate([r[1:], jnp.zeros_like(r[:1])], 0)
    lane = lax.broadcasted_iota(jnp.int32, r.shape, 2)
    return jnp.where(lane == LANES - 1, after, r)


def behind_z(x):
    r = pltpu.roll(x, 1, 2)
    before = jnp.concatenate([jnp.zeros_like(r[:1]), r[:-1]], 0)
    lane = lax.broadcasted_iota(jnp.int32, r.shape, 2)
    return jnp.where(lane == 0, before, r)


def kernel(
    tiles, sources,
    perm_ref, e_ref, h_ref, a_ref, b_ref,
    eout_ref, grad_ref,
    perm_in, e_in, h_in, a_in, b_in, e_last,
    coef, efield, hfield, ufield, bfield, halos, deltas, grad, parts,
    in_sem, out_sem, perm_send, perm_recv, grad_send, grad_recv, halo_send, halo_recv,
):
    count, ny, nz = perm_in.shape
    chunks = coef.shape[1]
    erows, hrows = pl.ds(0, ny), pl.ds(ROWS, ny)
    eahead, hbehind = pl.ds(1, ny), pl.ds(ROWS - 1, ny)
    rows = perm_ref.shape[0]
    tile = lax.axis_index("tile")
    me = lax.axis_index("src")
    has_below = tile > 0
    has_above = tile < tiles - 1
    own = pl.ds(me * rows, rows)

    loads = [
        pltpu.make_async_copy(e_ref.at[0], e_in, in_sem.at[0]),
        pltpu.make_async_copy(h_ref.at[0], h_in, in_sem.at[1]),
        pltpu.make_async_copy(perm_ref, perm_in.at[own], in_sem.at[2]),
        pltpu.make_async_copy(a_ref.at[0], a_in, in_sem.at[3]),
        pltpu.make_async_copy(b_ref.at[0], b_in, in_sem.at[4]),
    ]
    for copy in loads:
        copy.start()

    nothing = jnp.zeros((chunks, ny, LANES), jnp.float32)
    for c in (1, 2):
        efield[c, count, :, erows] = nothing
        hfield[c, 0, :, hrows] = nothing
        bfield[c, 0, :, hrows] = nothing
        for t in range(STEPS - 1):
            ufield[t, c, count, :, erows] = nothing

    def clear(p, carry):
        margin = jnp.zeros((chunks, ROWS, LANES), jnp.float32)
        for c in (0, 2):
            efield[c, p, :, pl.ds(ny, ROWS)] = margin
            hfield[c, p + 1, :, pl.ds(0, ROWS)] = margin
            bfield[c, p + 1, :, pl.ds(0, ROWS)] = margin
            for t in range(STEPS - 1):
                ufield[t, c, p, :, pl.ds(ny, ROWS)] = margin
        return carry

    lax.fori_loop(0, count, clear, 0)

    barrier = pltpu.get_barrier_semaphore()
    for d in range(1, sources):
        pl.semaphore_signal(
            barrier, 1, device_id={"tile": tile, "src": lax.rem(me + d, sources)}, device_id_type=MESH
        )

    @pl.when(has_below)
    def _():
        pl.semaphore_signal(barrier, 1, device_id={"tile": tile - 1, "src": me}, device_id_type=MESH)

    @pl.when(has_above)
    def _():
        pl.semaphore_signal(barrier, 1, device_id={"tile": tile + 1, "src": me}, device_id_type=MESH)

    ends = jnp.where(has_below, 1, 0) + jnp.where(has_above, 1, 0)
    pl.semaphore_wait(barrier, sources - 1 + ends)

    def perm_copy(d):
        return pltpu.make_async_remote_copy(
            src_ref=perm_ref,
            dst_ref=perm_in.at[own],
            send_sem=perm_send.at[d - 1],
            recv_sem=perm_recv.at[d - 1],
            device_id={"tile": tile, "src": lax.rem(me + d, sources)},
            device_id_type=MESH,
        )

    for d in range(1, sources):
        perm_copy(d).start()

    def pad(ref, index, start, value):
        for j in range(chunks):
            part = value[:, j * LANES : (j + 1) * LANES]
            have = part.shape[1]
            at = index + (j, pl.ds(start, ny))
            if have == LANES:
                ref[at] = part
            else:
                ref[at + (pl.ds(0, have),)] = part
                ref[at + (pl.ds(have, LANES - have),)] = jnp.zeros((ny, LANES - have), jnp.float32)

    def unpad(value, j):
        return value[..., : min(LANES, nz - j * LANES)]

    def down(ref, slot, c):
        return pltpu.make_async_remote_copy(
            src_ref=ref.at[c, 0, :, erows],
            dst_ref=halos.at[slot, c - 1],
            send_sem=halo_send.at[slot, c - 1],
            recv_sem=halo_recv.at[slot, c - 1],
            device_id={"tile": tile - 1, "src": me},
            device_id_type=MESH,
        )

    def up(ref, slot, c):
        return pltpu.make_async_remote_copy(
            src_ref=ref.at[c, count, :, hrows],
            dst_ref=halos.at[slot, c - 1],
            send_sem=halo_send.at[slot, c - 1],
            recv_sem=halo_recv.at[slot, c - 1],
            device_id={"tile": tile + 1, "src": me},
            device_id_type=MESH,
        )

    def send_down(ref, slot, c):
        @pl.when(has_below)
        def _():
            down(ref, slot, c).start()

    def send_up(ref, slot, c):
        @pl.when(has_above)
        def _():
            up(ref, slot, c).start()

    def sent_down(ref, slot):
        @pl.when(has_below)
        def _():
            for c in (2, 1):
                down(ref, slot, c).wait_send()

    def sent_up(ref, slot):
        @pl.when(has_above)
        def _():
            for c in (1, 2):
                up(ref, slot, c).wait_send()

    def step_h(es, hs):
        def run(base, group):
            e1, e2 = es[1, base, :, erows], es[2, base, :, erows]
            for j in range(group):
                p = base + j
                e0 = es[0, p, :, erows]
                n1, n2 = es[1, p + 1, :, erows], es[2, p + 1, :, erows]
                hs[0, p + 1, :, hrows] -= (es[2, p, :, eahead] - e2) - (ahead_z(e1) - e1)
                hs[1, p + 1, :, hrows] -= (ahead_z(e0) - e0) - (n2 - e2)
                hs[2, p + 1, :, hrows] -= (n1 - e1) - (es[0, p, :, eahead] - e0)
                e1, e2 = n1, n2

        over_planes(0, count, MOST, run)

    def edge_h(es, hs, slot_in, slot_out):
        for c, other, sign in ((1, 2, 1.0), (2, 1, -1.0)):
            @pl.when(has_above)
            def _():
                down(es, slot_in, other).wait_recv()
                hs[c, count, :, hrows] += sign * halos[slot_in, other - 1]

            send_up(hs, slot_out, c)

    def step_e(hs, put):
        def run(base, group):
            m1, m2 = hs[1, base, :, hrows], hs[2, base, :, hrows]
            for p in [base + j for j in range(group)]:
                h0, h1, h2 = (hs[c, p + 1, :, hrows] for c in range(3))
                k = coef[p]
                put(
                    p,
                    (
                        k * ((h2 - hs[2, p + 1, :, hbehind]) - (h1 - behind_z(h1))),
                        k * ((h0 - behind_z(h0)) - (h2 - m2)),
                        k * ((h1 - m1) - (h0 - hs[0, p + 1, :, hbehind])),
                    ),
                )
                m1, m2 = h1, h2

        over_planes(0, count, MOST, run)

    def edge_e(hs, slot_in, fix, send):
        for c, other, sign in ((2, 1, -1.0), (1, 2, 1.0)):
            @pl.when(has_below)
            def _():
                up(hs, slot_in, other).wait_recv()
                fix(c, sign * (coef[0] * halos[slot_in, other - 1]))

            send(c)

    half = STEPS // 2

    def dot(left, right):
        return left[0] * right[0] + left[1] * right[1] + left[2] * right[2]

    def put_last(c, p, value):
        for j in range(chunks):
            part = unpad(value[j], j)
            e_last[c, p, :, pl.ds(j * LANES, part.shape[1])] = part

    def forward(t):
        def put(p, d):
            for c in range(3):
                if t == STEPS:
                    put_last(c, p, efield[c, p, :, erows] + d[c])
                else:
                    efield[c, p, :, erows] += d[c]
                if t <= half:
                    deltas[t, c, p] = d[c]
            if t > half:
                grad[p] += dot(d, [ufield[STEPS - t, c, p, :, erows] for c in range(3)])

        def fix(c, d):
            if t == STEPS:
                for j in range(chunks):
                    part = unpad(d[j], j)
                    e_last[c, 0, :, pl.ds(j * LANES, part.shape[1])] += part
            else:
                efield[c, 0, :, erows] += d
            if t <= half:
                deltas[t, c, 0] += d
            else:
                grad[0] += d * ufield[STEPS - t, c, 0, :, erows]

        return put, fix

    def adjoint(t):
        def put(p, d):
            u = tuple(ufield[t - 1, c, p, :, erows] + d[c] for c in range(3))
            if t < STEPS - 1:
                for c in range(3):
                    ufield[t, c, p, :, erows] = u[c]
            if t >= half:
                term = dot(u, [deltas[STEPS - t, c, p] for c in range(3)])
                grad[p] = term if t == half else grad[p] + term

        def fix(c, d):
            if t < STEPS - 1:
                ufield[t, c, 0, :, erows] += d
            if t >= half:
                grad[0] += d * deltas[STEPS - t, c, 0]

        return put, fix

    MOST = 8

    loads[0].wait()

    def prepare_e(base, group):
        for p in [base + j for j in range(group)]:
            for c in range(3):
                pad(efield, (c, p), 0, e_in[c, p])

    prepare_e(0, 1)
    for c in (2, 1):
        send_down(efield, 0, c)
    over_planes(1, count - 1, 3, prepare_e)
    loads[1].wait()

    def prepare_h(base, group):
        for p in [base + j for j in range(group)]:
            for c in range(3):
                pad(hfield, (c, p + 1), ROWS, h_in[c, p] * (1.0 / COURANT))

    over_planes(0, count, 2, prepare_h)
    step_h(efield, hfield)
    edge_h(efield, hfield, 0, 1)

    loads[4].wait()

    def prepare_b(base, group):
        for p in [base + j for j in range(group)]:
            for c in range(3):
                pad(bfield, (c, p + 1), ROWS, b_in[c, p] * (-1.0 / COURANT))

    over_planes(0, count, 2, prepare_b)
    loads[2].wait()
    loads[3].wait()
    for d in range(1, sources):
        perm_copy(d).wait_recv()

    def prepare_u(base, group):
        for p in [base + j for j in range(group)]:
            inverse = 1.0 / perm_in[p]
            pad(coef, (p,), 0, inverse * (COURANT * COURANT))
            for c in range(3):
                pad(ufield, (0, c, p), 0, inverse * a_in[c, p])

    prepare_u(0, 1)
    for c in (2, 1):
        send_down(ufield.at[0], 2, c)
    over_planes(1, count - 1, 3, prepare_u)

    def grad_copy(d):
        peer = lax.rem(me + d, sources)
        return pltpu.make_async_remote_copy(
            src_ref=grad.at[pl.ds(peer * rows, rows)],
            dst_ref=parts.at[d - 1],
            send_sem=grad_send.at[d - 1],
            recv_sem=grad_recv.at[d - 1],
            device_id={"tile": tile, "src": peer},
            device_id_type=MESH,
        )

    for t in range(1, STEPS + 1):
        last = t == STEPS
        before = ufield.at[min(t, STEPS - 1) - 1]
        put, fix = forward(t)
        sent_down(efield, 0)
        step_e(hfield, put)
        if not last:
            if t > 1:
                sent_up(bfield, 3)
            step_h(before, bfield)
        else:
            for d in range(1, sources):
                @pl.when(lax.rem(me + d, sources) != 0)
                def _():
                    grad_copy(d).start()

            pltpu.make_async_copy(
                e_last.at[:, pl.ds(1, count - 1)], eout_ref.at[0, :, pl.ds(1, count - 1)], out_sem.at[0]
            ).start()
        edge_e(hfield, 1, fix, lambda c: None if last else send_down(efield, 0, c))
        if last:
            break
        edge_h(before, bfield, 2, 3)
        put, fix = adjoint(t)
        sent_up(hfield, 1)
        step_h(efield, hfield)
        sent_down(before, 2)
        step_e(bfield, put)
        edge_h(efield, hfield, 0, 1)
        edge_e(bfield, 3, fix, lambda c: send_down(ufield.at[t], 2, c) if t < STEPS - 1 else None)

    for d in range(1, sources):
        @pl.when(lax.rem(me + d, sources) == 0)
        def _():
            grad_copy(d).start()

    tail = pltpu.make_async_copy(
        e_last.at[:, pl.ds(0, 1)], eout_ref.at[0, :, pl.ds(0, 1)], out_sem.at[1]
    )
    tail.start()
    sent_up(hfield, 1)
    sent_up(bfield, 3)
    total = grad[own]
    for d in range(1, sources):
        grad_copy(d).wait_recv()
        total = total + parts[d - 1]
    for j in range(chunks):
        part = unpad(total[:, j], j)
        grad_ref[:, :, pl.ds(j * LANES, part.shape[2])] = -part
    for d in range(1, sources):
        perm_copy(d).wait_send()
        grad_copy(d).wait_send()
    pltpu.make_async_copy(
        e_last.at[:, pl.ds(1, count - 1)], eout_ref.at[0, :, pl.ds(1, count - 1)], out_sem.at[0]
    ).wait()
    tail.wait()


def hand_over(e_ref, grad_ref, eout_ref, gout_ref, sem):
    first = e_ref.shape[2] // 2
    copies = [pltpu.make_async_copy(grad_ref, gout_ref, sem.at[6])]
    for c in range(3):
        for i, planes in enumerate((pl.ds(0, first), pl.ds(first, e_ref.shape[2] - first))):
            copies.append(
                pltpu.make_async_copy(
                    e_ref.at[0, c, planes], eout_ref.at[0, c, planes], sem.at[2 * c + i]
                )
            )
    for copy in copies:
        copy.start()
    for copy in copies:
        copy.wait()


def on_device(tiles, sources, permittivity, e_start, h_start, e_cotangent, h_cotangent):
    rows, ny, nz = permittivity.shape
    count = rows * sources
    chunks = -(-nz // LANES)
    any_spec = pl.BlockSpec(memory_space=pltpu.HBM)
    vmem = lambda *shape: pltpu.VMEM(shape, jnp.float32)
    dma = lambda n: pltpu.SemaphoreType.DMA((n,))
    efinal, gradient = pl.pallas_call(
        functools.partial(kernel, tiles, sources),
        out_shape=(
            jax.ShapeDtypeStruct(e_start.shape, jnp.float32),
            jax.ShapeDtypeStruct(permittivity.shape, jnp.float32),
        ),
        in_specs=[any_spec] * 5,
        out_specs=(any_spec, pl.BlockSpec(memory_space=pltpu.VMEM)),
        scratch_shapes=[
            vmem(count, ny, nz),
            vmem(3, count, ny, nz),
            vmem(3, count, ny, nz),
            vmem(3, count, ny, nz),
            vmem(3, count, ny, nz),
            vmem(3, count, ny, nz),
            vmem(count, chunks, ny, LANES),
            vmem(3, count + 1, chunks, ny + ROWS, LANES),
            vmem(3, count + 1, chunks, ny + ROWS, LANES),
            vmem(STEPS - 1, 3, count + 1, chunks, ny + ROWS, LANES),
            vmem(3, count + 1, chunks, ny + ROWS, LANES),
            vmem(4, 2, chunks, ny, LANES),
            vmem(STEPS // 2 + 1, 3, count, chunks, ny, LANES),
            vmem(count, chunks, ny, LANES),
            vmem(sources - 1, rows, chunks, ny, LANES),
            dma(5),
            dma(2),
            dma(sources - 1),
            dma(sources - 1),
            dma(sources - 1),
            dma(sources - 1),
            pltpu.SemaphoreType.DMA((4, 2)),
            pltpu.SemaphoreType.DMA((4, 2)),
        ],
        compiler_params=pltpu.CompilerParams(
            collective_id=0, has_side_effects=True, vmem_limit_bytes=60 * 1024 * 1024
        ),
    )(permittivity, e_start, h_start, e_cotangent, h_cotangent)
    hbm_spec = pl.BlockSpec(memory_space=pltpu.HBM)
    return pl.pallas_call(
        hand_over,
        out_shape=(
            jax.ShapeDtypeStruct(efinal.shape, jnp.float32),
            jax.ShapeDtypeStruct(gradient.shape, jnp.float32),
        ),
        in_specs=[hbm_spec, hbm_spec],
        out_specs=(hbm_spec, hbm_spec),
        scratch_shapes=[dma(2 * 3 + 1)],
        compiler_params=pltpu.CompilerParams(vmem_limit_bytes=60 * 1024 * 1024),
    )(efinal, gradient)


def solution(mesh):
    fields = P("src", None, "tile", None, None)
    cells = P(("tile", "src"), None, None)
    return jax.shard_map(
        functools.partial(on_device, mesh.shape["tile"], mesh.shape["src"]),
        mesh=mesh,
        in_specs=(cells, fields, fields, fields, fields),
        out_specs=(fields, cells),
        check_vma=False,
    )
```
